32 devices in a mesh: tile: 4 (over z), tensor: 8 (over y, x, core).
Axes of the slice: x: 2, y: 2, z: 4, core: 2. Of those that a mesh axis runs over, the one named last changes fastest.
Arguments:
- image_hidden: bfloat16 [8, 32, 32, 3072], P(None, 'tile', 'tensor'), may hold values from -6 to 6
- text_hidden: bfloat16 [8, 512, 3072], P(None, ('tile', 'tensor')), may hold values from -6 to 6
- latents: float32 [8, 32, 2048], P(None, 'tile', 'tensor'), may hold values from -6 to 6
- step_index: int32 [8], replicated, may hold values from 0 to 27
- anchor: int32 [8, 2], replicated, may hold values from 0 to 63
- text_len: int32 [8], replicated, may hold values from 64 to 512
- mod_image: float32 [8, 3, 3072], replicated, may hold values from -3 to 3
- mod_text: float32 [8, 3, 3072], replicated, may hold values from -3 to 3
- mod_mlp: float32 [8, 3, 3072], replicated, may hold values from -3 to 3
- mod_final: float32 [8, 2, 3072], replicated, may hold values from -3 to 3
- qkv_image: bfloat16 [3072, 3, 2048], P(None, None, 'tensor'), may hold values from -0.109375 to 0.109375
- qkv_text: bfloat16 [3072, 3, 2048], P(None, None, 'tensor'), may hold values from -0.109375 to 0.109375
- proj_image: bfloat16 [2048, 3072], P('tensor'), may hold values from -0.125 to 0.125
- proj_text: bfloat16 [2048, 3072], P('tensor'), may hold values from -0.125 to 0.125
- qk_gain: float32 [2, 2, 128], replicated, may hold values from 0.5 to 10
- mlp_expand: bfloat16 [3072, 6144], P(None, 'tensor'), may hold values from -0.109375 to 0.109375
- mlp_reduce: bfloat16 [6144, 3072], P('tensor'), may hold values from -0.078125 to 0.078125
- final_weight: bfloat16 [3072, 64], replicated, may hold values from -0.109375 to 0.109375
Outputs:
- image_out: bfloat16 [8, 32, 32, 3072], P(None, 'tile', 'tensor')
- text_out: bfloat16 [8, 512, 3072], P(None, ('tile', 'tensor'))
- latents_ext: float32 [8, 40, 2048], P(None, 'tile', 'tensor')
The draws below stay inside these ranges and needn't reach their ends.
Inputs may be any that keep to these rules, and one draw needn't show every extreme that they name: text_len gives each request's live text tokens; slots at or past it take no part as keys. step_index is a step of the 28-step plan.
All inputs are finite; a program needn't handle non-finite values.
Results may differ from the reference program's by a relative error of at most 0.0085.
The reference program's roundings to bfloat16 on the way (of `image_mod`, `text_mod`, `probs`, `attended`, `mlp_mod`, `activated` and `final_in`) count: a program that leaves them out, or rounds other values in their place, can miss the bound.
Values may be sent and summed in bfloat16 or wider, within the bound.
A program may use at most 128 MiB of HBM per device.

```python
import math
import jax
import jax.numpy as jnp
from jax import lax

D = 3072
HEADS = 16
HEAD_DIM = 128
MLP = 6144
C = 64
GRID = 32
L_TXT = 512
REQS = 8
NSTEPS = 28
N_TILE = 4


def draw_qk_gain(key, part):
    base_key = jax.random.fold_in(key, 0)
    gains = jax.random.uniform(base_key, (2, 2, HEAD_DIM), jnp.float32, 0.5, 3.2)
    return gains


def touch_ends(drawn, key, low, top_value):
    place = [jax.random.randint(jax.random.fold_in(key, axis), (), 0, length) for axis, length in enumerate(drawn.shape)]
    widest = drawn.shape.index(max(drawn.shape))
    beside = place[:widest] + [(place[widest] + 1) % drawn.shape[widest]] + place[widest + 1:]
    return drawn.at[tuple(place)].set(low).at[tuple(beside)].set(top_value)


def steps_of(key, shape, cuts, least, high):
    def one(axis_at, parts):
        draws = jax.random.uniform(jax.random.fold_in(jax.random.fold_in(key, 6), axis_at), (parts,), jnp.float32, least / len(cuts), high / len(cuts))
        return jnp.repeat(jnp.exp(draws), shape[axis_at] // parts).reshape((-1,) + (1,) * (len(shape) - axis_at - 1))

    level = one(*cuts[0])
    for cut in cuts[1:]:
        level = level * one(*cut)
    return level


def normal_values(key, dims, deviation, limit, cuts=(), kind=jnp.bfloat16):
    values = deviation * jax.random.normal(key, dims, jnp.float32)
    if cuts:
        values = values * steps_of(key, dims, cuts, -0.22, 0.18)
    return jnp.clip(values, -limit, limit).astype(kind)


def setup_inputs(seed: int = 0) -> dict:
    key_of = jax.random.split(jax.random.key(seed), 19)
    image_hidden = normal_values(key_of[0], (REQS, GRID, GRID, D), 1.0, 6.0, ((1, 4), (2, 8)))
    text_hidden = normal_values(key_of[1], (REQS, L_TXT, D), 1.0, 6.0, ((1, 32),))
    latents = normal_values(key_of[2], (REQS, GRID, GRID * C), 1.0, 6.0, ((1, 4), (2, 8)), jnp.float32)
    step_index = touch_ends(jax.random.randint(key_of[3], (REQS,), 0, NSTEPS), jax.random.fold_in(key_of[3], 1), 0, NSTEPS - 1).astype(jnp.int32)
    anchor = touch_ends(jax.random.randint(key_of[4], (REQS, 2), 0, 64), jax.random.fold_in(key_of[4], 1), 0, 63).astype(jnp.int32)
    text_len = touch_ends(jax.random.randint(key_of[5], (REQS,), 64, L_TXT + 1), jax.random.fold_in(key_of[5], 1), 64, L_TXT).astype(jnp.int32)
    mod_image = normal_values(key_of[6], (REQS, 3, D), 0.5, 3.0, (), jnp.float32)
    mod_text = normal_values(key_of[7], (REQS, 3, D), 0.5, 3.0, (), jnp.float32)
    mod_mlp = normal_values(key_of[8], (REQS, 3, D), 0.5, 3.0, (), jnp.float32)
    mod_final = normal_values(key_of[9], (REQS, 2, D), 0.5, 3.0, (), jnp.float32)
    qkv_image = normal_values(key_of[10], (D, 3, HEADS * HEAD_DIM), D ** -0.5, 0.109375, ((2, 8),))
    qkv_text = normal_values(key_of[11], (D, 3, HEADS * HEAD_DIM), D ** -0.5, 0.109375, ((2, 8),))
    proj_image = normal_values(key_of[12], (HEADS * HEAD_DIM, D), (HEADS * HEAD_DIM) ** -0.5, 0.125, ((0, 8),))
    proj_text = normal_values(key_of[13], (HEADS * HEAD_DIM, D), (HEADS * HEAD_DIM) ** -0.5, 0.125, ((0, 8),))
    qk_gain = draw_qk_gain(jax.random.fold_in(key_of[18], 71), 0)
    mlp_expand = normal_values(key_of[15], (D, MLP), D ** -0.5, 0.109375, ((1, 8),))
    mlp_reduce = normal_values(key_of[16], (MLP, D), MLP ** -0.5, 0.078125, ((0, 8),))
    final_weight = normal_values(key_of[17], (D, C), D ** -0.5, 0.109375)
    return {"image_hidden": image_hidden, "text_hidden": text_hidden, "latents": latents, "step_index": step_index, "anchor": anchor, "text_len": text_len, "mod_image": mod_image, "mod_text": mod_text, "mod_mlp": mod_mlp, "mod_final": mod_final, "qkv_image": qkv_image, "qkv_text": qkv_text, "proj_image": proj_image, "proj_text": proj_text, "qk_gain": qk_gain, "mlp_expand": mlp_expand, "mlp_reduce": mlp_reduce, "final_weight": final_weight}


norm_eps = 1e-06
time_shift = 3.0

def layer_norm(values):
    average = lax.optimization_barrier(jnp.mean(values, -1, keepdims=True))
    centred = values - average
    spread = lax.optimization_barrier(jnp.mean(centred * centred, -1, keepdims=True))
    return centred * lax.rsqrt(spread + norm_eps)

def modulate(hidden, shift, stretch):
    normed = layer_norm(hidden.astype(jnp.float32))
    return ((1.0 + stretch) * normed + shift).astype(jnp.bfloat16)

def rope_tables(row_ids, col_ids):
    pair_index = jnp.arange(64, dtype=jnp.int32)
    row_rank = (pair_index - 8).astype(jnp.float32)
    col_rank = (pair_index - 36).astype(jnp.float32)
    log_base = math.log(10000.0)
    row_freq = jnp.where((pair_index >= 8) & (pair_index < 36), jnp.exp(-2.0 * row_rank / 56.0 * log_base), 0.0).astype(jnp.float32)
    col_freq = jnp.where(pair_index >= 36, jnp.exp(-2.0 * col_rank / 56.0 * log_base), 0.0).astype(jnp.float32)
    angles = row_ids[..., None] * row_freq + col_ids[..., None] * col_freq
    angles = jnp.repeat(angles, 2, axis=-1)
    sign_table = jnp.where(jnp.arange(128, dtype=jnp.int32) % 2 == 0, -1.0, 1.0).astype(jnp.float32)
    return (jnp.cos(angles), jnp.sin(angles) * sign_table)

def rotate(values, cos_table, sin_table):
    paired = values.reshape(values.shape[:-1] + (values.shape[-1] // 2, 2))
    swapped = jnp.flip(paired, -1).reshape(values.shape)
    return values * cos_table + swapped * sin_table

def head_norm(projected, head_gain):
    squares = lax.optimization_barrier(jnp.mean(projected * projected, -1, keepdims=True))
    return projected * lax.rsqrt(squares + norm_eps) * head_gain

def sigma_of(step_float):
    level = 1.0 - step_float / NSTEPS
    return time_shift * level / (1.0 + (time_shift - 1.0) * level)

def reference(image_hidden, text_hidden, latents, step_index, anchor, text_len, mod_image, mod_text, mod_mlp, mod_final, qkv_image, qkv_text, proj_image, proj_text, qk_gain, mlp_expand, mlp_reduce, final_weight):
    requests = image_hidden.shape[0]
    model_width = image_hidden.shape[3]
    image_count = GRID * GRID
    image_mod = modulate(image_hidden, mod_image[:, 0, None, None, :], mod_image[:, 1, None, None, :]).reshape(requests * image_count, model_width)
    text_mod = modulate(text_hidden, mod_text[:, 0, None, :], mod_text[:, 1, None, :]).reshape(requests * L_TXT, model_width)
    token_index = jnp.arange(image_count, dtype=jnp.int32)
    row_ids = (anchor[:, 0:1] + token_index[None, :] // GRID).astype(jnp.float32)
    col_ids = (anchor[:, 1:2] + token_index[None, :] % GRID).astype(jnp.float32)
    cos_table, sin_table = rope_tables(row_ids, col_ids)
    key_pos = jnp.arange(L_TXT + image_count, dtype=jnp.int32)
    usable = jnp.logical_or(key_pos[None, :] >= L_TXT, key_pos[None, :] < text_len[:, None])
    score_scale = 1.0 / math.sqrt(HEAD_DIM)
    image_heads = qkv_image.reshape(model_width, 3, HEADS, HEAD_DIM).transpose(2, 0, 1, 3).reshape(HEADS, model_width, 3 * HEAD_DIM)
    text_heads = qkv_text.reshape(model_width, 3, HEADS, HEAD_DIM).transpose(2, 0, 1, 3).reshape(HEADS, model_width, 3 * HEAD_DIM)
    image_projs = proj_image.reshape(HEADS, HEAD_DIM, model_width)
    text_projs = proj_text.reshape(HEADS, HEAD_DIM, model_width)

    def one_head(sums, weights):
        image_sum, text_sum = sums
        image_w, text_w, image_p, text_p = weights
        image_qkv = jnp.dot(image_mod, image_w, preferred_element_type=jnp.float32).reshape(requests, image_count, 3, HEAD_DIM)
        text_qkv = jnp.dot(text_mod, text_w, preferred_element_type=jnp.float32).reshape(requests, L_TXT, 3, HEAD_DIM)
        query = jnp.concatenate([head_norm(text_qkv[:, :, 0], qk_gain[1, 0]).astype(jnp.bfloat16), rotate(head_norm(image_qkv[:, :, 0], qk_gain[0, 0]), cos_table, sin_table).astype(jnp.bfloat16)], 1)
        keys = jnp.concatenate([head_norm(text_qkv[:, :, 1], qk_gain[1, 1]).astype(jnp.bfloat16), rotate(head_norm(image_qkv[:, :, 1], qk_gain[0, 1]), cos_table, sin_table).astype(jnp.bfloat16)], 1)
        values = jnp.concatenate([text_qkv[:, :, 2], image_qkv[:, :, 2]], 1).astype(jnp.bfloat16)
        scores = jnp.einsum('rqd,rkd->rqk', query.astype(jnp.float32), keys.astype(jnp.float32)) * score_scale
        masked = jnp.where(usable[:, None, :], scores, -jnp.inf)
        row_top = lax.optimization_barrier(jnp.max(masked, -1, keepdims=True))
        weights_raw = jnp.where(usable[:, None, :], jnp.exp(scores - row_top), 0.0)
        weight_sum = lax.optimization_barrier(jnp.sum(weights_raw, -1, keepdims=True))
        probs = weights_raw.astype(jnp.bfloat16)
        attended = (jnp.einsum('rqk,rkd->rqd', probs.astype(jnp.float32), values.astype(jnp.float32)) / weight_sum).astype(jnp.bfloat16)
        text_sum = text_sum + jnp.dot(attended[:, :L_TXT].reshape(requests * L_TXT, HEAD_DIM), text_p, preferred_element_type=jnp.float32)
        image_sum = image_sum + jnp.dot(attended[:, L_TXT:].reshape(requests * image_count, HEAD_DIM), image_p, preferred_element_type=jnp.float32)
        return ((image_sum, text_sum), None)
    start_sums = (jnp.zeros((requests * image_count, model_width), jnp.float32), jnp.zeros((requests * L_TXT, model_width), jnp.float32))
    (image_sum, text_sum), unused = lax.scan(one_head, start_sums, (image_heads, text_heads, image_projs, text_projs))
    image_mid = (image_hidden.astype(jnp.float32) + mod_image[:, 2, None, None, :] * image_sum.reshape(requests, GRID, GRID, model_width)).astype(jnp.bfloat16)
    text_out = (text_hidden.astype(jnp.float32) + mod_text[:, 2, None, :] * text_sum.reshape(requests, L_TXT, model_width)).astype(jnp.bfloat16)
    mlp_mod = modulate(image_mid, mod_mlp[:, 0, None, None, :], mod_mlp[:, 1, None, None, :]).reshape(requests * image_count, model_width)
    activated = jax.nn.gelu(jnp.dot(mlp_mod, mlp_expand, preferred_element_type=jnp.float32), approximate=True).astype(jnp.bfloat16)
    mlp_sum = jnp.dot(activated, mlp_reduce, preferred_element_type=jnp.float32).reshape(requests, GRID, GRID, model_width)
    image_out = (image_mid.astype(jnp.float32) + mod_mlp[:, 2, None, None, :] * mlp_sum).astype(jnp.bfloat16)
    final_in = modulate(image_out, mod_final[:, 0, None, None, :], mod_final[:, 1, None, None, :])
    velocity = jnp.dot(final_in.reshape(requests * image_count, model_width), final_weight, preferred_element_type=jnp.float32).reshape(requests, GRID, GRID * C)
    step_float = step_index.astype(jnp.float32)
    time_delta = sigma_of(step_float + 1.0) - sigma_of(step_float)
    latents_next = latents + time_delta[:, None, None] * velocity
    padded = jnp.pad(latents_next, ((0, 0), (1, 1), (0, 0)))
    tile_rows = GRID // N_TILE
    row_pick = (jnp.arange(N_TILE, dtype=jnp.int32)[:, None] * tile_rows + jnp.arange(tile_rows + 2, dtype=jnp.int32)[None, :]).reshape(-1)
    latents_ext = padded[:, row_pick, :]
    return (image_out, text_out, latents_ext)
```

```python
import math

import jax
import jax.numpy as jnp
from jax import lax
from jax.experimental import pallas as pl
from jax.experimental.pallas import tpu as pltpu
from jax.sharding import PartitionSpec as P

HEAD_DIM = 128
GRID = 32
NSTEPS = 28
CHUNKS = 2


norm_eps = 1e-06
time_shift = 3.0


def padded(value, sides, width):
    for axis, dim in sides:
        size, length = (lax.axis_size(axis), value.shape[dim])
        up = [(i, (i + 1) % size) for i in range(size - 1)]
        down = [(j, i) for i, j in up]
        last = lax.slice_in_dim(value, length - width, length, axis=dim)
        leading = lax.slice_in_dim(value, 0, width, axis=dim)
        before = lax.ppermute(last, axis, up)
        after = lax.ppermute(leading, axis, down)
        value = jnp.concatenate([before, value, after], axis=dim)
    return value


def layer_norm(values):
    average = jnp.mean(values, -1, keepdims=True)
    centred = values - average
    spread = jnp.mean(centred * centred, -1, keepdims=True)
    return centred * lax.rsqrt(spread + norm_eps)


def modulate(hidden, shift, stretch):
    normed = layer_norm(hidden.astype(jnp.float32))
    return ((1.0 + stretch) * normed + shift).astype(jnp.bfloat16)


def rope_tables(row_ids, col_ids):
    pair_index = jnp.arange(64, dtype=jnp.int32)
    row_rank = (pair_index - 8).astype(jnp.float32)
    col_rank = (pair_index - 36).astype(jnp.float32)
    log_base = math.log(10000.0)
    row_freq = jnp.where(
        (pair_index >= 8) & (pair_index < 36), jnp.exp(-2.0 * row_rank / 56.0 * log_base), 0.0
    )
    col_freq = jnp.where(pair_index >= 36, jnp.exp(-2.0 * col_rank / 56.0 * log_base), 0.0)
    angles = row_ids[..., None] * row_freq + col_ids[..., None] * col_freq
    cos_half, sin_half = jnp.cos(angles), jnp.sin(angles)
    return (
        jnp.concatenate([cos_half, cos_half], -1),
        jnp.concatenate([-sin_half, sin_half], -1),
    )


def sigma_of(step_float):
    level = 1.0 - step_float / NSTEPS
    return time_shift * level / (1.0 + (time_shift - 1.0) * level)


def norm_rotate_kernel(heads, image_ref, text_ref, cos_ref, sin_ref, gain_ref, out_ref):
    text_count = text_ref.shape[2]
    image_count = image_ref.shape[2]

    def head_norm(values, gain):
        squares = jnp.mean(values * values, -1, keepdims=True)
        return values * lax.rsqrt(squares + norm_eps) * gain

    for r in range(image_ref.shape[1]):
        cos_table = cos_ref[0, r]
        sin_table = sin_ref[0, r]
        for kind in range(3):
            for h in range(heads):
                at = (kind * heads + h) * HEAD_DIM
                image = image_ref[0, r, :, at : at + HEAD_DIM]
                text = text_ref[0, r, :, at : at + HEAD_DIM]
                if kind < 2:
                    image = head_norm(image, gain_ref[kind : kind + 1, :])
                    text = head_norm(text, gain_ref[2 + kind : 3 + kind, :])
                    image = image * cos_table + pltpu.roll(image, HEAD_DIM // 2, 1) * sin_table
                out_ref[r, kind, h, 0, :text_count, :] = text.astype(jnp.bfloat16)
                out_ref[r, kind, h, 0, text_count : text_count + image_count, :] = image.astype(
                    jnp.bfloat16
                )


def norm_rotate(image_qkv, text_qkv, cos_table, sin_table, gains, heads):
    parts, requests, image_count, width = image_qkv.shape
    text_count = text_qkv.shape[2]
    count = image_count + text_count

    def rows(n, w):
        return pl.BlockSpec((1, requests, n, w), lambda i: (i, 0, 0, 0))

    return pl.pallas_call(
        lambda *refs: norm_rotate_kernel(heads, *refs),
        grid=(parts,),
        out_shape=jax.ShapeDtypeStruct(
            (requests, 3, heads, parts, count, HEAD_DIM), jnp.bfloat16
        ),
        in_specs=[
            rows(image_count, width),
            rows(text_count, width),
            rows(image_count, HEAD_DIM),
            rows(image_count, HEAD_DIM),
            pl.BlockSpec((4, HEAD_DIM), lambda i: (0, 0)),
        ],
        out_specs=pl.BlockSpec(
            (requests, 3, heads, 1, count, HEAD_DIM), lambda i: (0, 0, 0, i, 0, 0)
        ),
        compiler_params=pltpu.CompilerParams(vmem_limit_bytes=32 * 1024 * 1024),
        cost_estimate=pl.CostEstimate(
            flops=12 * parts * requests * count * width,
            bytes_accessed=6 * parts * requests * count * width,
            transcendentals=0,
        ),
    )(image_qkv, text_qkv, cos_table, sin_table, gains)


def split_pairs(weight, heads):
    width, _, cols = weight.shape
    place = jnp.arange(HEAD_DIM, dtype=jnp.int32)
    source = (place % (HEAD_DIM // 2)) * 2 + place // (HEAD_DIM // 2)
    one_head = (place[:, None] == source[None, :]).astype(jnp.bfloat16)
    block = jnp.kron(jnp.eye(2 * heads, dtype=jnp.bfloat16), one_head)
    flat = weight.reshape(width, 3 * cols)
    moved = jnp.dot(flat[:, : 2 * cols], block, preferred_element_type=jnp.float32)
    return jnp.concatenate([moved.astype(jnp.bfloat16), flat[:, 2 * cols :]], 1)


def rotated_pairs(size, step):
    return [(i, (i + step) % size) for i in range(size)]


def attend(query, keys, values, owners, text_len, text_count, part_count, tile_text):
    offset = jnp.arange(keys.shape[2] // len(owners), dtype=jnp.int32)
    part, inner = offset // part_count, offset % part_count
    local = jnp.where(inner < text_count, part * text_count + inner, -1)
    text_pos = jnp.concatenate(
        [jnp.where(local < 0, -1, owner * tile_text + local) for owner in owners]
    )
    usable = (text_pos[None, :] < text_len[:, None])[:, None, None, :]
    score_scale = 1.0 / math.sqrt(HEAD_DIM)
    scores = (
        jnp.einsum("rhqd,rhkd->rhqk", query, keys, preferred_element_type=jnp.float32)
        * score_scale
    )
    row_top = jnp.max(jnp.where(usable, scores, -jnp.inf), -1, keepdims=True)
    weights = jnp.where(usable, jnp.exp(scores - row_top), 0.0)
    weight_sum = jnp.sum(weights, -1, keepdims=True)
    accum = jnp.einsum(
        "rhqk,rhkd->rhqd",
        weights.astype(jnp.bfloat16),
        values,
        preferred_element_type=jnp.float32,
    )
    return (accum / weight_sum).astype(jnp.bfloat16)


def per_device(
    image_hidden,
    text_hidden,
    latents,
    step_index,
    anchor,
    text_len,
    mod_image,
    mod_text,
    mod_mlp,
    mod_final,
    qkv_image,
    qkv_text,
    proj_image,
    proj_text,
    qk_gain,
    mlp_expand,
    mlp_reduce,
    final_weight,
):
    all_requests, tile_rows, tile_cols, model_width = image_hidden.shape
    local_cols = qkv_image.shape[2]
    heads = local_cols // HEAD_DIM
    local_units = mlp_expand.shape[1]
    tiles = lax.axis_size("tile")
    parts = lax.axis_size("tensor")
    tile_index = lax.axis_index("tile")
    text_count = text_hidden.shape[1]
    image_count = tile_rows * tile_cols
    part_count = text_count + image_count
    by_request = all_requests % tiles == 0
    chunks = CHUNKS if all_requests % (CHUNKS * tiles) == 0 else 1
    requests = all_requests // chunks
    own = requests // tiles

    image_w = split_pairs(qkv_image, heads)
    text_w = split_pairs(qkv_text, heads)
    gains = qk_gain.reshape(4, HEAD_DIM // 2, 2).transpose(0, 2, 1).reshape(4, HEAD_DIM)
    part_index = jnp.arange(parts, dtype=jnp.int32)[:, None, None]
    token = jnp.arange(image_count, dtype=jnp.int32)[None, None, :]
    row_ids = anchor[None, :, 0:1] + tile_index * tile_rows + token // tile_cols + 0 * part_index
    col_ids = anchor[None, :, 1:2] + part_index * tile_cols + token % tile_cols
    cos_table, sin_table = rope_tables(row_ids.astype(jnp.float32), col_ids.astype(jnp.float32))
    step_float = step_index.astype(jnp.float32)
    time_delta = sigma_of(step_float + 1.0) - sigma_of(step_float)

    def rows_of(value, c):
        return value[c * requests : (c + 1) * requests]

    def gather(value):
        return lax.all_gather(value, "tensor", axis=0, tiled=False)

    def scatter(value):
        return lax.psum_scatter(value, "tensor", scatter_dimension=0, tiled=False)

    def exchange_attend(joint, lengths):
        blocks, owners = [], []
        for step in range(tiles):
            to = lax.rem(tile_index + step, tiles)
            block = lax.dynamic_slice_in_dim(joint, to * own, own, 0)
            if step:
                block = lax.ppermute(block, "tile", rotated_pairs(tiles, step))
            blocks.append(block)
            owners.append(lax.rem(tile_index + tiles - step, tiles))
        whole = jnp.concatenate(blocks, 3)
        attended = attend(
            whole[:, 0],
            whole[:, 1],
            whole[:, 2],
            owners,
            lax.dynamic_slice_in_dim(lengths, tile_index * own, own, 0),
            text_count,
            part_count,
            text_count * parts,
        )
        count = parts * part_count
        back = []
        for step in range(tiles):
            block = attended[:, :, step * count : (step + 1) * count]
            if step:
                block = lax.ppermute(block, "tile", rotated_pairs(tiles, tiles - step))
            back.append(block)
        return lax.dynamic_slice_in_dim(
            jnp.concatenate(back + back, 0),
            lax.rem(tiles - tile_index, tiles) * own,
            requests,
            0,
        )

    hidden, text, gathered = [], [], []
    for c in range(chunks):
        image_c = rows_of(image_hidden, c).reshape(requests, image_count, model_width)
        text_c = rows_of(text_hidden, c)
        mi, mt = rows_of(mod_image, c), rows_of(mod_text, c)
        hidden.append(image_c)
        text.append(text_c)
        gathered.append(
            (
                gather(modulate(text_c, mt[:, 0, None, :], mt[:, 1, None, :])),
                gather(modulate(image_c, mi[:, 0, None, :], mi[:, 1, None, :])),
            )
        )

    image_sums, text_sums = [], []
    for c in range(chunks):
        text_mod, image_mod = gathered[c]
        text_qkv = jnp.dot(
            text_mod.reshape(-1, model_width), text_w, preferred_element_type=jnp.float32
        ).reshape(parts, requests, text_count, 3 * local_cols)
        image_qkv = jnp.dot(
            image_mod.reshape(-1, model_width), image_w, preferred_element_type=jnp.float32
        ).reshape(parts, requests, image_count, 3 * local_cols)
        in_chunk = slice(c * requests, (c + 1) * requests)
        joint = norm_rotate(
            image_qkv, text_qkv, cos_table[:, in_chunk], sin_table[:, in_chunk], gains, heads
        ).reshape(requests, 3, heads, parts * part_count, HEAD_DIM)
        if by_request:
            attended = exchange_attend(joint, rows_of(text_len, c))
        else:
            every = lax.all_gather(joint[:, 1:], "tile", axis=3, tiled=True)
            attended = attend(
                joint[:, 0],
                every[:, 0],
                every[:, 1],
                list(range(tiles)),
                rows_of(text_len, c),
                text_count,
                part_count,
                text_count * parts,
            )
        ordered = attended.reshape(requests, heads, parts, part_count, HEAD_DIM)
        ordered = ordered.transpose(2, 0, 3, 1, 4).reshape(parts, requests, part_count, local_cols)
        image_term = jnp.dot(
            ordered[:, :, text_count:].reshape(-1, local_cols),
            proj_image,
            preferred_element_type=jnp.float32,
        ).astype(jnp.bfloat16)
        image_sums.append(scatter(image_term.reshape(parts, requests, image_count, model_width)))
        text_sums.append((ordered, c))

    mids, mods = [], []
    for c in range(chunks):
        gate = rows_of(mod_image, c)[:, 2, None, :]
        mm = rows_of(mod_mlp, c)
        image_mid = (
            hidden[c].astype(jnp.float32) + gate * image_sums[c].astype(jnp.float32)
        ).astype(jnp.bfloat16)
        mids.append(image_mid)
        mods.append(gather(modulate(image_mid, mm[:, 0, None, :], mm[:, 1, None, :])))

    image_outs, text_outs, nexts = [], [], []
    for c in range(chunks):
        mm = rows_of(mod_mlp, c)
        mf = rows_of(mod_final, c)
        ordered, _ = text_sums[c]
        text_term = jnp.dot(
            ordered[:, :, :text_count].reshape(-1, local_cols),
            proj_text,
            preferred_element_type=jnp.float32,
        ).astype(jnp.bfloat16)
        text_sum = scatter(text_term.reshape(parts, requests, text_count, model_width))
        text_outs.append(
            (
                text[c].astype(jnp.float32)
                + rows_of(mod_text, c)[:, 2, None, :] * text_sum.astype(jnp.float32)
            ).astype(jnp.bfloat16)
        )
        grown = jnp.dot(
            mods[c].reshape(-1, model_width), mlp_expand, preferred_element_type=jnp.float32
        )
        activated = jax.nn.gelu(grown, approximate=True).astype(jnp.bfloat16)
        mlp_term = jnp.dot(activated, mlp_reduce, preferred_element_type=jnp.float32).astype(
            jnp.bfloat16
        )
        mlp_sum = scatter(mlp_term.reshape(parts, requests, image_count, model_width))
        image_out = (
            mids[c].astype(jnp.float32) + mm[:, 2, None, :] * mlp_sum.astype(jnp.float32)
        ).astype(jnp.bfloat16)
        image_outs.append(image_out)
        final_in = modulate(image_out, mf[:, 0, None, :], mf[:, 1, None, :])
        velocity = jnp.dot(
            final_in.reshape(-1, model_width), final_weight, preferred_element_type=jnp.float32
        ).reshape(requests, tile_rows, tile_cols * final_weight.shape[1])
        nexts.append(rows_of(latents, c) + rows_of(time_delta, c)[:, None, None] * velocity)

    image_out = jnp.concatenate(image_outs, 0).reshape(image_hidden.shape)
    text_out = jnp.concatenate(text_outs, 0)
    latents_ext = padded(jnp.concatenate(nexts, 0), (("tile", 1),), 1)
    return (image_out, text_out, latents_ext)


def solution(mesh):
    return jax.shard_map(
        per_device,
        mesh=mesh,
        in_specs=(
            P(None, "tile", "tensor", None),
            P(None, ("tile", "tensor"), None),
            P(None, "tile", "tensor"),
            P(),
            P(),
            P(),
            P(),
            P(),
            P(),
            P(),
            P(None, None, "tensor"),
            P(None, None, "tensor"),
            P("tensor", None),
            P("tensor", None),
            P(),
            P(None, "tensor"),
            P("tensor", None),
            P(),
        ),
        out_specs=(
            P(None, "tile", "tensor", None),
            P(None, ("tile", "tensor"), None),
            P(None, "tile", "tensor"),
        ),
        check_vma=False,
    )
```
